256 devices in a mesh: lat: 32 (over z, x), lyr: 4 (over y_lo, core), dp: 2 (over y_hi).
Axes of the slice: x: 4, y: 4 (y_hi: 2, y_lo: 2; y = y_hi * 2 + y_lo), z: 8, core: 2. Of those that a mesh axis runs over, the one named last changes fastest.
Arguments:
- act_codes: bfloat16 [1024, 4, 4096], P('dp', 'lyr'), may hold values from -6 to 6
- act_scales: bfloat16 [1024, 4, 32], P('dp', 'lyr'), may hold values from 0.25 to 2.5
- latents: bfloat16 [1024, 16384], P('dp', 'lat'), may hold values from 0 to 36, as said below
- dec_weight: bfloat16 [16384, 4, 4096], P('lat', 'lyr', 'dp'), may hold values from -0.296875 to 0.296875
- dec_bias: float32 [4, 4096], P('lyr'), may hold values from -3 to 3
Outputs:
- grad_enc: float32 [4096, 4, 16384], P('dp', 'lyr', 'lat')
- grad_dec: float32 [16384, 4, 4096], P('lat', 'lyr', 'dp')
- grad_bias: float32 [16384], P('lat')
The draws below stay inside these ranges and needn't reach their ends.
Inputs may be any that keep to these rules, and one draw needn't show every extreme that they name: `latents`: nonnegative, with many exact zeros.
All inputs are finite; a program needn't handle non-finite values.
Results may differ from the reference program's by a relative error of at most 0.00065.
The reference program's roundings to bfloat16 on the way (of `inputs_bf`, `resid` and `grad_pre`) count: a program that leaves them out, or rounds other values in their place, can miss the bound.
Values may be sent and summed in bfloat16 or wider, within the bound.
A program may use at most 192 MiB of HBM per device.

```python
import math
import jax
import jax.numpy as jnp
from jax import lax

D = 4096
LATENTS = 16384
LAYERS = 4
ROWS = 1024
BLOCKS = 32


def draw_latents(key, part):
    key = jax.random.fold_in(key, 5)
    k_base, k_rows, k_cols = jax.random.split(key, 3)
    raw_values = jnp.clip(jax.random.normal(k_base, (ROWS, LATENTS)), -4.0, 4.0)
    row_scale = jnp.exp(jax.random.uniform(k_rows, (ROWS, 1), minval=math.log(0.3), maxval=math.log(3.0)))
    col_scale = jnp.exp(jax.random.uniform(k_cols, (1, LATENTS), minval=math.log(0.3), maxval=math.log(3.0)))
    return (jnp.maximum(raw_values, 0.0) * row_scale * col_scale).astype(jnp.bfloat16)


def draw_dec_weight(key, part):
    key = jax.random.fold_in(key, 9)
    k_base, k_rows, k_cols = jax.random.split(key, 3)
    raw_values = jnp.clip(jax.random.normal(k_base, (LATENTS, LAYERS, D)), -4.0, 4.0)
    row_scale = jnp.exp(jax.random.uniform(k_rows, (LATENTS, LAYERS, 1), minval=math.log(0.3), maxval=math.log(3.0)))
    col_scale = jnp.exp(jax.random.uniform(k_cols, (1, 1, D), minval=math.log(0.3), maxval=math.log(3.0)))
    values = raw_values * row_scale * col_scale / math.sqrt(LATENTS)
    return jnp.clip(values, -0.296875, 0.296875).astype(jnp.bfloat16)


def block_scale(rng, shape, cuts, low, high):
    factor_of, own = 1.0, jax.random.fold_in(rng, 6)
    for position, shards_of in cuts:
        steps = jnp.exp(jax.random.uniform(jax.random.fold_in(own, position), (shards_of,), jnp.float32, low / len(cuts), high / len(cuts)))
        factor_of = factor_of * jnp.repeat(steps, shape[position] // shards_of).reshape([-1 if axis == position else 1 for axis in range(len(shape))])
    return factor_of


def gaussian(rng, shape, scale, bound, cuts=(), held_as=jnp.bfloat16):
    result = scale * jax.random.normal(rng, shape, jnp.float32)
    if cuts:
        result = result * block_scale(rng, shape, cuts, -0.22, 0.18)
    return jnp.clip(result, -bound, bound).astype(held_as)


def setup_inputs(seed: int = 0) -> dict:
    streams_of = jax.random.split(jax.random.key(seed), 6)
    act_codes = gaussian(streams_of[0], (ROWS, LAYERS, D), 1.0, 6.0, ((0, 2), (1, 4)))
    act_scales = jnp.clip(jnp.exp(math.log(2.5) - 2.3025851 * jax.random.uniform(streams_of[1], (ROWS, LAYERS, BLOCKS), jnp.float32) ** block_scale(streams_of[1], (ROWS, LAYERS, BLOCKS), ((0, 2), (1, 4)), -0.2, 0.2)), 0.25, 2.5).astype(jnp.bfloat16)
    latents = draw_latents(jax.random.fold_in(streams_of[5], 71), 0)
    dec_weight = draw_dec_weight(jax.random.fold_in(streams_of[5], 71), 0)
    dec_bias = gaussian(streams_of[4], (LAYERS, D), 0.5, 3.0, ((0, 4),), jnp.float32)
    return dict(act_codes=act_codes, act_scales=act_scales, latents=latents, dec_weight=dec_weight, dec_bias=dec_bias)


penalty = 1.0
epsilon = 1e-06

def dequantize(code_block, scale_block):
    row_count, layer_count, width = code_block.shape
    block_count = scale_block.shape[2]
    scaled = code_block.astype(jnp.float32).reshape(row_count, layer_count, block_count, width // block_count) * scale_block.astype(jnp.float32)[..., None]
    return scaled.reshape(row_count, layer_count, width)

def reference(act_codes, act_scales, latents, dec_weight, dec_bias):
    inputs = dequantize(act_codes, act_scales)
    inputs_bf = inputs.astype(jnp.bfloat16)
    norm_list = []
    resid_list = []
    grad_act = jnp.zeros((latents.shape[0], latents.shape[1]), jnp.float32)
    for layer in range(LAYERS):
        weight_layer = dec_weight[:, layer, :]
        wide = weight_layer.astype(jnp.float32)
        norm_list.append(jnp.sqrt(lax.optimization_barrier(jnp.sum(wide * wide, axis=1)) + epsilon))
        recon = jnp.dot(latents, weight_layer, preferred_element_type=jnp.float32)
        resid = (recon + dec_bias[layer][None, :] - inputs[:, layer, :]).astype(jnp.bfloat16)
        resid_list.append(resid)
        grad_act = grad_act + jnp.dot(resid, weight_layer.T, preferred_element_type=jnp.float32)
    row_norms = jnp.stack(norm_list, axis=1)
    norm_total = lax.optimization_barrier(jnp.sum(row_norms, axis=1))
    grad_act = grad_act + penalty * norm_total[None, :]
    grad_pre = jnp.where(latents > 0, grad_act, 0.0).astype(jnp.bfloat16)
    grad_bias = lax.optimization_barrier(jnp.sum(grad_pre.astype(jnp.float32), axis=0))
    act_sum = lax.optimization_barrier(jnp.sum(latents.astype(jnp.float32), axis=0))
    enc_list = []
    dec_list = []
    for layer in range(LAYERS):
        enc_list.append(jnp.dot(inputs_bf[:, layer, :].T, grad_pre, preferred_element_type=jnp.float32))
        scaled_rows = (penalty * act_sum / row_norms[:, layer])[:, None] * dec_weight[:, layer, :].astype(jnp.float32)
        dec_list.append(jnp.dot(latents.T, resid_list[layer], preferred_element_type=jnp.float32) + scaled_rows)
    grad_enc = jnp.stack(enc_list, axis=1)
    grad_dec = jnp.stack(dec_list, axis=1)
    return (grad_enc, grad_dec, grad_bias)
```

```python
import jax
import jax.numpy as jnp
from jax import lax
from jax.sharding import PartitionSpec as P

penalty = 1.0
epsilon = 1e-06


def dequantize(code_block, scale_block):
    rows, width = code_block.shape
    blocks = scale_block.shape[1]
    scaled = (
        code_block.astype(jnp.float32).reshape(rows, blocks, width // blocks)
        * scale_block.astype(jnp.float32)[..., None]
    )
    return scaled.reshape(rows, width)


def swap_halves(block, half):
    width = block.shape[1] // 2
    kept = lax.dynamic_slice_in_dim(block, half * width, width, 1)
    given = lax.dynamic_slice_in_dim(block, (1 - half) * width, width, 1)
    got = lax.ppermute(given, "dp", [(0, 1), (1, 0)])
    first = jnp.where(half == 0, kept, got)
    second = jnp.where(half == 0, got, kept)
    return jnp.concatenate([first, second], axis=0)


def shards(act_codes, act_scales, latents, dec_weight, dec_bias):
    half = lax.axis_index("dp")
    lat_id = lax.axis_index("lat")
    weight = dec_weight[:, 0, :]
    width = weight.shape[1]
    wide = weight.astype(jnp.float32)
    acts = lax.all_gather(latents, "dp", axis=0, tiled=True)
    codes = swap_halves(act_codes[:, 0, :], half)
    scales = swap_halves(act_scales[:, 0, :], half)
    bias = lax.dynamic_slice_in_dim(dec_bias, half * width, width, 1)

    partial_value = jnp.dot(acts, weight, preferred_element_type=jnp.float32)
    recon = lax.psum_scatter(partial_value, "lat", scatter_dimension=0, tiled=True)
    part = recon.shape[0]
    my_inputs = dequantize(
        lax.dynamic_slice_in_dim(codes, lat_id * part, part, 0),
        lax.dynamic_slice_in_dim(scales, lat_id * part, part, 0),
    )
    resid_part = (recon + bias - my_inputs).astype(jnp.bfloat16)
    resid = lax.all_gather(resid_part, "lat", axis=0, tiled=True)

    squares = lax.psum(jnp.sum(jnp.square(wide), axis=1), "dp")
    row_norms = jnp.sqrt(squares + epsilon)
    norm_total = lax.psum(row_norms, "lyr")
    act_sum = jnp.sum(acts.astype(jnp.float32), axis=0)

    grad_part = jnp.dot(resid, weight.T, preferred_element_type=jnp.float32)
    grad_sum = lax.psum_scatter(grad_part, ("lyr", "dp"), scatter_dimension=0, tiled=True)
    rows = grad_sum.shape[0]
    place = lax.axis_index("lyr") * 2 + half
    my_acts = lax.dynamic_slice_in_dim(acts, place * rows, rows, 0)
    pre_part = jnp.where(my_acts > 0, grad_sum + penalty * norm_total[None, :], 0.0).astype(
        jnp.bfloat16
    )
    grad_pre = lax.all_gather(pre_part, ("lyr", "dp"), axis=0, tiled=True)

    scaled_rows = (penalty * act_sum / row_norms)[:, None] * wide
    grad_dec = (
        lax.dot_general(acts, resid, (((0,), (0,)), ((), ())), preferred_element_type=jnp.float32)
        + scaled_rows
    )
    inputs_bf = dequantize(codes, scales).astype(jnp.bfloat16)
    grad_enc = lax.dot_general(
        inputs_bf, grad_pre, (((0,), (0,)), ((), ())), preferred_element_type=jnp.float32
    )
    grad_bias = jnp.sum(grad_pre.astype(jnp.float32), axis=0)
    return (grad_enc[:, None, :], grad_dec[:, None, :], grad_bias)


def solution(mesh):
    in_specs = (
        P("dp", "lyr", None),
        P("dp", "lyr", None),
        P("dp", "lat"),
        P("lat", "lyr", "dp"),
        P("lyr", None),
    )
    out_specs = (P("dp", "lyr", "lat"), P("lat", "lyr", "dp"), P("lat"))
    return jax.shard_map(shards, mesh=mesh, in_specs=in_specs, out_specs=out_specs, check_vma=False)
```

```python
import functools

import jax
import jax.numpy as jnp
from jax import lax
from jax.experimental import pallas as pl
from jax.experimental.pallas import tpu as pltpu
from jax.sharding import PartitionSpec as P

penalty = 1.0
epsilon = 1e-06
MESH = pl.DeviceIdType.MESH
f32, bf16 = jnp.float32, jnp.bfloat16

ROWS, FB, WIDTH = 1024, 512, 2048
HALF = WIDTH // 2
PIECE = HALF // 4
NT = (((1,), (1,)), ((), ()))
TN = (((0,), (0,)), ((), ()))


def aligned(value, step):
    return pl.multiple_of(value, step)


def spread(scales, first, width):
    blocks = scales.shape[0]
    row = lax.broadcasted_iota(jnp.int32, (blocks, width), 0)
    col = lax.broadcasted_iota(jnp.int32, (blocks, width), 1)
    pick = jnp.where(row == first + col // 128, 1.0, 0.0).astype(bf16)
    return lax.dot_general(scales, pick, TN, preferred_element_type=f32)


def exchange_kernel(
    lat, w, sc, bias, codes,
    resid_o, acts_o, pre_o, sq_o, codes_o, sc_o,
    la, wx, part, rs, resid, grad, grad_in, grad_y, pre, mine_codes, other_codes, sq_mine, sq_other, sc_other,
    local_sem, l1s, l1r, wss, wsr, l2s, l2r, l3s, l3r, rss, rsr, xs_, xr_, z0s, z0r, z1s, z1r, x1s, x1r,
    gcs, gcr, gys, gyr, pys, pyr, pcs, pcr, ms, mr, cs, cr,
):
    lat_id = lax.axis_index("lat")
    lyr = lax.axis_index("lyr")
    h = lax.axis_index("dp")
    x, z = lat_id % 4, lat_id // 4
    ylo, c = lyr // 2, lyr % 2
    y = h * 2 + ylo

    def at(xx=x, yy=y, zz=z, cc=c):
        return (zz * 4 + xx, (yy % 2) * 2 + cc, yy // 2)

    xp = [(x + o) % 4 for o in range(4)]
    yp = [(y + o) % 4 for o in range(4)]
    zr, zl = (z + 1) % 8, (z + 7) % 8
    sibling = at(cc=1 - c)
    partner = at(yy=yp[2])

    def rcopy(src, dst, send, recv, device):
        return pltpu.make_async_remote_copy(
            src_ref=src, dst_ref=dst, send_sem=send, recv_sem=recv, device_id=device, device_id_type=MESH
        )

    barrier = pltpu.get_barrier_semaphore()
    neighbours = [at(xx=xp[o]) for o in (1, 2, 3)] + [at(yy=yp[o]) for o in (1, 2, 3)]
    neighbours += [at(zz=zr), at(zz=zl), sibling]
    for d in neighbours:
        pl.semaphore_signal(barrier, inc=1, device_id=d, device_id_type=MESH)
    pl.semaphore_wait(barrier, len(neighbours))

    sends = []
    my_block = aligned((y * 2 + c) * 128, 128)
    my_cols = aligned(x * FB, FB)

    own = aligned((ylo * 2 + c) * 128, 128)
    l1 = []
    for o in (1, 2, 3):
        cp = rcopy(
            lat.at[pl.ds(own, 128), :],
            la.at[pl.ds(my_block, 128), pl.ds(my_cols, FB)],
            l1s.at[o - 1], l1r.at[o - 1], at(xx=xp[o]),
        )
        cp.start()
        l1.append(cp)
    wcopies = [[], []]
    for k in range(2):
        for o in (1, 2, 3):
            cols = aligned(k * HALF + xp[o] * PIECE, PIECE)
            cp = rcopy(
                w.at[:, pl.ds(cols, PIECE)],
                wx.at[k, pl.ds(my_cols, FB), :],
                wss.at[k, o - 1], wsr.at[k, o - 1], at(xx=xp[o]),
            )
            cp.start()
            wcopies[k].append(cp)
    row0 = aligned((z % 4) * 128, 128)
    misc = []
    for k in range(2):
        theirs = aligned((1 - h) * WIDTH + k * HALF + x * PIECE, PIECE)
        cp = rcopy(codes.at[pl.ds(row0, 128), pl.ds(theirs, PIECE)], other_codes.at[k], ms.at[k], mr.at[k], partner)
        cp.start()
        misc.append(cp)
        ours = aligned(h * WIDTH + k * HALF + x * PIECE, PIECE)
        cp = pltpu.make_async_copy(
            codes.at[pl.ds(row0, 128), pl.ds(ours, PIECE)], mine_codes.at[k], local_sem.at[k]
        )
        cp.start()
        misc.append(cp)
    cp = rcopy(sc.at[pl.ds(aligned((1 - h) * 16, 16), 16), :], sc_other, ms.at[2], mr.at[2], partner)
    cp.start()
    misc.append(cp)

    la[pl.ds(my_block, 128), pl.ds(my_cols, FB)] = lat[pl.ds(own, 128), :]
    for k in range(2):
        cols = aligned(k * HALF + x * PIECE, PIECE)
        wx[k, pl.ds(my_cols, FB), :] = w[:, pl.ds(cols, PIECE)]

    ones = jnp.ones((8, WIDTH), bf16)

    @pl.loop(0, 4)
    def _(i):
        at_f = aligned(i * 128, 128)
        wide = w[pl.ds(at_f, 128), :].astype(f32)
        square = wide * wide
        high = square.astype(bf16)
        low = (square - high.astype(f32)).astype(bf16)
        sq_mine[:, pl.ds(at_f, 128)] = lax.dot_general(
            ones, high, NT, preferred_element_type=f32
        ) + lax.dot_general(ones, low, NT, preferred_element_type=f32)

    cp = rcopy(sq_mine, sq_other, ms.at[3], mr.at[3], partner)
    cp.start()
    misc.append(cp)

    for cp in l1:
        cp.wait_recv()
    l2 = {}
    block = la.at[pl.ds(my_block, 128), :]
    l3 = []
    cp = rcopy(block, block, l3s.at[0], l3r.at[0], sibling)
    cp.start()
    l3.append(cp)
    for o in (1, 3, 2):
        cp = rcopy(block, block, l2s.at[o - 1], l2r.at[o - 1], at(yy=yp[o]))
        cp.start()
        l2[o] = cp

    def dots(chunk, k):
        rows = aligned(chunk * 256, 256)
        part[k, pl.ds(rows, 256), :] = jnp.dot(
            la[pl.ds(rows, 256), :], wx[k], preferred_element_type=f32
        )

    l3[0].wait_recv()
    for k in range(2):
        for cp in wcopies[k]:
            cp.wait_recv()

    @pl.loop(0, 2)
    def _(k):
        dots(y, k)

    for i, o in enumerate((3, 1, 2)):
        source = (y + 4 - o) % 4
        l2[o].wait_recv()
        arrived = la.at[pl.ds(aligned((source * 2 + c) * 128, 128), 128), :]
        cp = rcopy(arrived, arrived, l3s.at[i + 1], l3r.at[i + 1], sibling)
        cp.start()
        l3.append(cp)
        cp.wait_recv()

        @pl.loop(0, 2)
        def _(k, source=source):
            dots(source, k)

    code_copies = []
    theirs = aligned((1 - h) * WIDTH, WIDTH)
    for i in range(4):
        cp = rcopy(
            codes.at[pl.ds(i * 128, 128), pl.ds(theirs, WIDTH)],
            codes_o.at[pl.ds(i * 128, 128), :],
            cs.at[i], cr.at[i], partner,
        )
        cp.start()
        code_copies.append(cp)

    def local_part(k, s, owner):
        return part[k, pl.ds(aligned(owner * 128 + s * 64, 64), 64), :]

    def ring_owner(s, step):
        return (z + 15 - step) % 8 if s == 0 else (z + 1 + step) % 8

    ring = {}
    for k in range(2):
        for s in range(2):
            cp = rcopy(
                part.at[k, pl.ds(aligned(ring_owner(s, 0) * 128 + s * 64, 64), 64), :],
                rs.at[k, s, 0], rss.at[k, s, 0], rsr.at[k, s, 0], at(zz=zr if s == 0 else zl),
            )
            cp.start()
            ring[k, s, 0] = cp
    for step in range(1, 7):
        for k in range(2):
            for s in range(2):
                ring[k, s, step - 1].wait_recv()
                rs[k, s, step - 1] += local_part(k, s, ring_owner(s, step))
                cp = rcopy(
                    rs.at[k, s, step - 1], rs.at[k, s, step],
                    rss.at[k, s, step], rsr.at[k, s, step], at(zz=zr if s == 0 else zl),
                )
                cp.start()
                ring[k, s, step] = cp

    for cp in misc:
        cp.wait()
    is_own = (z // 4) == h
    my_scales = jnp.where(
        is_own,
        sc[pl.ds(aligned(h * 16, 16), 16), pl.ds(row0, 128)].astype(f32),
        sc_other[:, pl.ds(row0, 128)].astype(f32),
    ).astype(bf16)
    x_cols = aligned(x * PIECE, PIECE)
    z_rows = aligned(z * 128, 128)
    x0, x1 = [], {}
    for k in range(2):
        wide_codes = jnp.where(is_own, mine_codes[k].astype(f32), other_codes[k].astype(f32))
        inputs = wide_codes * spread(my_scales, k * 8 + x * 2, PIECE)
        shift = bias[:, pl.ds(aligned(h * WIDTH + k * HALF + x * PIECE, PIECE), PIECE)]
        for s in range(2):
            ring[k, s, 6].wait_recv()
            recon = rs[k, s, 6] + local_part(k, s, z)
            value = (recon + shift - inputs[s * 64 : s * 64 + 64, :]).astype(bf16)
            resid[k, pl.ds(aligned(z * 128 + s * 64, 64), 64), pl.ds(x_cols, PIECE)] = value
        if k == 0:
            tile = resid.at[0, pl.ds(z_rows, 128), pl.ds(x_cols, PIECE)]
            for o in (1, 2, 3):
                cp = rcopy(tile, tile, xs_.at[o - 1], xr_.at[o - 1], at(xx=xp[o]))
                cp.start()
                x0.append(cp)

    def send_z(k, sems, rows, count, step, way):
        cols = pl.ds(0, HALF) if k == 0 else pl.ds(x_cols, PIECE)
        tile = resid.at[k, pl.ds(rows, count), cols]
        cp = rcopy(tile, tile, sems[0].at[way, step], sems[1].at[way, step], at(zz=zr if way == 0 else zl))
        cp.start()
        return cp

    def send_x1(owner, index):
        tile = resid.at[1, pl.ds(aligned(owner * 128, 128), 128), pl.ds(x_cols, PIECE)]
        out = []
        for o in (1, 2, 3):
            cp = rcopy(tile, tile, x1s.at[index, o - 1], x1r.at[index, o - 1], at(xx=xp[o]))
            cp.start()
            out.append(cp)
        return out

    squares = sq_mine[0:1, :] + sq_other[0:1, :]
    sq_o[...] = jnp.broadcast_to(squares, sq_o.shape)
    half_norms = (0.5 * penalty) * jnp.sqrt(squares + epsilon)

    def grad_rows(first, count):
        rows = pl.ds(aligned(first, count), count)
        grad[rows, :] = (
            lax.dot_general(resid[0, rows, :], w[:, :HALF], NT, preferred_element_type=f32)
            + lax.dot_general(resid[1, rows, :], w[:, HALF:], NT, preferred_element_type=f32)
            + half_norms
        )

    zc = {}
    zc[1, 0, 0] = send_z(1, (z1s, z1r), z_rows, 128, 0, 0)
    zc[1, 1, 0] = send_z(1, (z1s, z1r), z_rows, 128, 0, 1)
    x1[0] = send_x1(z, 0)
    for cp in x0:
        cp.wait_recv()
    zc[0, 0, 0] = send_z(0, (z0s, z0r), z_rows, 128, 0, 0)
    zc[0, 1, 0] = send_z(0, (z0s, z0r), z_rows, 128, 0, 1)
    for cp in x1[0]:
        cp.wait_recv()
    grad_rows(z * 128, 128)
    for step in range(1, 5):
        for way in range(2):
            source = (z + 8 - step) % 8 if way == 0 else (z + step) % 8
            rows = aligned(source * 128, 128)
            count = 128
            if step == 4:
                rows, count = aligned(source * 128 + way * 64, 64), 64
            for k, sems in ((1, (z1s, z1r)), (0, (z0s, z0r))):
                zc[k, way, step - 1].wait_recv()
                if step < 3:
                    zc[k, way, step] = send_z(k, sems, rows, 128, step, way)
                elif step == 3:
                    zc[k, way, step] = send_z(k, sems, aligned(source * 128 + way * 64, 64), 64, step, way)
                if k == 1 and step < 4:
                    x1[step * 2 - 1 + way] = send_x1(source, step * 2 - 1 + way)
            if step < 4:
                for cp in x1[step * 2 - 1 + way]:
                    cp.wait_recv()
                grad_rows(source * 128, 128)
    x1[7] = send_x1((z + 4) % 8, 7)
    for cp in x1[7]:
        cp.wait_recv()
    grad_rows(((z + 4) % 8) * 128, 128)

    out_copies = [
        pltpu.make_async_copy(resid, resid_o, local_sem.at[2]),
        pltpu.make_async_copy(la.at[:, pl.ds(my_cols, FB)], acts_o, local_sem.at[3]),
    ]
    for cp in out_copies:
        cp.start()

    gc = []
    for o in (2, 1, 3, 0):
        rows = pl.ds(aligned((yp[o] * 2 + 1 - c) * 128, 128), 128)
        cp = rcopy(grad.at[rows, :], grad_in.at[o], gcs.at[o], gcr.at[o], sibling)
        cp.start()
        gc.append((o, cp))
    gy = []
    for o, cp in gc:
        cp.wait_recv()
        rows = pl.ds(aligned((yp[o] * 2 + c) * 128, 128), 128)
        grad_in[o] = grad_in[o] + grad[rows, :]
        if o:
            out = rcopy(grad_in.at[o], grad_y.at[o - 1], gys.at[o - 1], gyr.at[o - 1], at(yy=yp[o]))
            out.start()
            gy.append(out)
    total = grad_in[0]
    for cp in gy:
        cp.wait_recv()
    total = total + grad_y[0] + grad_y[1] + grad_y[2]
    active = la[pl.ds(my_block, 128), pl.ds(my_cols, FB)].astype(f32) > 0
    pre[pl.ds(my_block, 128), :] = jnp.where(active, total, 0.0).astype(bf16)
    tile = pre.at[pl.ds(my_block, 128), :]
    pc = [rcopy(tile, tile, pcs.at[0], pcr.at[0], sibling)]
    pc[0].start()
    py = {}
    for o in (2, 1, 3):
        py[o] = rcopy(tile, tile, pys.at[o - 1], pyr.at[o - 1], at(yy=yp[o]))
        py[o].start()
    for i, o in enumerate((1, 3, 2)):
        py[o].wait_recv()
        source = (y + 4 - o) % 4
        tile = pre.at[pl.ds(aligned((source * 2 + c) * 128, 128), 128), :]
        cp = rcopy(tile, tile, pcs.at[i + 1], pcr.at[i + 1], sibling)
        cp.start()
        pc.append(cp)
    for cp in pc:
        cp.wait_recv()
    pre_o[...] = pre[...]
    sc_o[...] = sc_other[...]

    for cp in code_copies:
        cp.wait()
    for cp in out_copies:
        cp.wait()
    for cp in l1 + wcopies[0] + wcopies[1] + list(l2.values()) + l3 + list(ring.values()) + x0:
        cp.wait_send()
    for cp in list(zc.values()) + sum(x1.values(), []) + [cp for _, cp in gc] + gy + list(py.values()) + pc:
        cp.wait_send()


def exchange(lat, w, sc, bias, codes):
    vmem = pl.BlockSpec(memory_space=pltpu.VMEM)
    hbm = pl.BlockSpec(memory_space=pl.ANY)
    dma = pltpu.SemaphoreType.DMA
    shape = jax.ShapeDtypeStruct
    return pl.pallas_call(
        exchange_kernel,
        out_shape=[
            shape((2, ROWS, HALF), bf16),
            shape((ROWS, FB), bf16),
            shape((ROWS, FB), bf16),
            shape((8, FB), f32),
            shape((ROWS // 2, WIDTH), bf16),
            shape((16, ROWS // 2), bf16),
        ],
        in_specs=[vmem, vmem, vmem, vmem, hbm],
        out_specs=[hbm, hbm, vmem, vmem, hbm, vmem],
        scratch_shapes=[
            pltpu.VMEM((ROWS, 4 * FB), bf16),
            pltpu.VMEM((2, 4 * FB, PIECE), bf16),
            pltpu.VMEM((2, ROWS, PIECE), f32),
            pltpu.VMEM((2, 2, 7, 64, PIECE), f32),
            pltpu.VMEM((2, ROWS, HALF), bf16),
            pltpu.VMEM((ROWS, FB), f32),
            pltpu.VMEM((4, 128, FB), f32),
            pltpu.VMEM((3, 128, FB), f32),
            pltpu.VMEM((ROWS, FB), bf16),
            pltpu.VMEM((2, 128, PIECE), bf16),
            pltpu.VMEM((2, 128, PIECE), bf16),
            pltpu.VMEM((8, FB), f32),
            pltpu.VMEM((8, FB), f32),
            pltpu.VMEM((16, ROWS // 2), bf16),
            dma((4,)),
            dma((3,)), dma((3,)),
            dma((2, 3)), dma((2, 3)),
            dma((3,)), dma((3,)),
            dma((4,)), dma((4,)),
            dma((2, 2, 7)), dma((2, 2, 7)),
            dma((3,)), dma((3,)),
            dma((2, 4)), dma((2, 4)),
            dma((2, 4)), dma((2, 4)),
            dma((8, 3)), dma((8, 3)),
            dma((4,)), dma((4,)),
            dma((3,)), dma((3,)),
            dma((3,)), dma((3,)),
            dma((4,)), dma((4,)),
            dma((4,)), dma((4,)),
            dma((4,)), dma((4,)),
        ],
        compiler_params=pltpu.CompilerParams(
            collective_id=0, has_side_effects=True, vmem_limit_bytes=50 * 2**20
        ),
        name="exchange",
    )(lat, w, sc, bias, codes)


def grads_kernel(half, acts, resid, w, pre, squares, own_codes, other_codes, own_sc, other_sc, enc_o, dec_o, bias_o):
    step = pl.program_id(0)
    h = half[0]
    act_sum = jnp.sum(acts[...].astype(f32), axis=0, keepdims=True)
    scale = penalty * act_sum / jnp.sqrt(squares[0:1, :] + epsilon)
    column = jnp.broadcast_to(scale, (128, 128)).T
    for k in range(2):
        term = lax.dot_general(acts[...], resid[k], TN, preferred_element_type=f32)
        for j in range(8):
            cols = slice(k * HALF + j * 128, k * HALF + j * 128 + 128)
            dec_o[pl.ds(k * 8 + j, 128, stride=16), :] = (
                term[:, j * 128 : j * 128 + 128] + column * w[:, cols].astype(f32)
            )
    own_at = pl.multiple_of(h * 512, 512)
    other_at = pl.multiple_of((1 - h) * 512, 512)
    own_in = (own_codes[...].astype(f32) * spread(own_sc[...], step * 4, 512)).astype(bf16)
    other_in = (other_codes[...].astype(f32) * spread(other_sc[...], step * 4, 512)).astype(bf16)
    enc = lax.dot_general(own_in, pre[pl.ds(own_at, 512), :], TN, preferred_element_type=f32)
    enc += lax.dot_general(other_in, pre[pl.ds(other_at, 512), :], TN, preferred_element_type=f32)
    for j in range(4):
        enc_o[pl.ds(j, 512, stride=4), :] = enc[:, j * 128 : j * 128 + 128]

    @pl.when(step == 0)
    def _():
        bias_o[...] = jnp.broadcast_to(jnp.sum(pre[...].astype(f32), axis=0, keepdims=True), bias_o.shape)


def grads(half, acts, resid, w, pre, squares, codes, other_codes, sc, other_sc):
    whole = lambda *shape: pl.BlockSpec(shape, lambda i, h: (0,) * len(shape))
    return pl.pallas_call(
        grads_kernel,
        grid_spec=pltpu.PrefetchScalarGridSpec(
            num_scalar_prefetch=1,
            grid=(4,),
            in_specs=[
                pl.BlockSpec((ROWS, 128), lambda i, h: (0, i)),
                whole(2, ROWS, HALF),
                pl.BlockSpec((128, WIDTH), lambda i, h: (i, 0)),
                whole(ROWS, FB),
                pl.BlockSpec((8, 128), lambda i, h: (0, i)),
                pl.BlockSpec((512, 512), lambda i, h: (0, h[0] * 4 + i)),
                pl.BlockSpec((512, 512), lambda i, h: (0, i)),
                pl.BlockSpec((16, 512), lambda i, h: (h[0], 0)),
                whole(16, 512),
            ],
            out_specs=[
                pl.BlockSpec((2048, 128), lambda i, h: (i, 0)),
                pl.BlockSpec((2048, 128), lambda i, h: (i, 0)),
                whole(8, FB),
            ],
        ),
        out_shape=[
            jax.ShapeDtypeStruct((WIDTH * 4, 128), f32),
            jax.ShapeDtypeStruct((FB * 16, 128), f32),
            jax.ShapeDtypeStruct((8, FB), f32),
        ],
        compiler_params=pltpu.CompilerParams(vmem_limit_bytes=50 * 2**20),
        name="grads",
    )(half, acts, resid, w, pre, squares, codes, other_codes, sc, other_sc)


def shards(act_codes, act_scales, latents, dec_weight, dec_bias):
    w = dec_weight[:, 0, :]
    codes = act_codes[:, 0, :]
    sc = act_scales[:, 0, :].T
    resid, acts, pre, squares, other_codes, other_sc = exchange(latents, w, sc, dec_bias, codes)
    half = lax.axis_index("dp").astype(jnp.int32).reshape(1)
    enc, dec, bias = grads(half, acts, resid, w, pre, squares, codes, other_codes, sc, other_sc)
    return enc.reshape(WIDTH, 1, FB), dec.reshape(FB, 1, WIDTH), bias[0]


def solution(mesh):
    in_specs = (
        P("dp", "lyr", None),
        P("dp", "lyr", None),
        P("dp", "lat"),
        P("lat", "lyr", "dp"),
        P("lyr", None),
    )
    out_specs = (P("dp", "lyr", "lat"), P("lat", "lyr", "dp"), P("lat"))
    return jax.shard_map(shards, mesh=mesh, in_specs=in_specs, out_specs=out_specs, check_vma=False)
```

```python
import functools

import jax
import jax.numpy as jnp
from jax import lax
from jax.experimental import pallas as pl
from jax.experimental.pallas import tpu as pltpu
from jax.sharding import PartitionSpec as P

penalty = 1.0
epsilon = 1e-06
MESH = pl.DeviceIdType.MESH
f32, bf16 = jnp.float32, jnp.bfloat16

ROWS, FB, WIDTH = 1024, 512, 2048
HALF = WIDTH // 2
PIECE = HALF // 4
NT = (((1,), (1,)), ((), ()))
TN = (((0,), (0,)), ((), ()))


def aligned(value, step):
    return pl.multiple_of(value, step)


def spread(scales, first, width):
    blocks = scales.shape[0]
    row = lax.broadcasted_iota(jnp.int32, (blocks, width), 0)
    col = lax.broadcasted_iota(jnp.int32, (blocks, width), 1)
    pick = jnp.where(row == first + col // 128, 1.0, 0.0).astype(bf16)
    return lax.dot_general(scales, pick, TN, preferred_element_type=f32)


class Copies:
    def __init__(self):
        self.started = []

    def start(self, src, dst, sems, index, device):
        cp = pltpu.make_async_remote_copy(
            src_ref=src,
            dst_ref=dst,
            send_sem=sems[0].at[index],
            recv_sem=sems[1].at[index],
            device_id=device,
            device_id_type=MESH,
        )
        cp.start()
        self.started.append(cp)
        return cp

    def finish(self):
        for cp in self.started:
            cp.wait_send()


def exchange_kernel(
    lat, w_hbm, sc, bias, codes,
    resid_o, acts_o, pre_o, sq_o, codes_o, sc_o,
    la, w, wx, part, rs, resid, grad, core_in, core_sum, y_in, pre, mine_codes, other_codes, sq_mine, sq_other, sc_other,
    local_sem,
    l1a, l1b, wa, wb, l2a, l2b, l3a, l3b, rsa, rsb, x0a, x0b, z0a, z0b, z1a, z1b, x1a, x1b,
    gca, gcb, gya, gyb, pya, pyb, pca, pcb, ma, mb, ca, cb,
):
    lat_id = lax.axis_index("lat")
    lyr = lax.axis_index("lyr")
    h = lax.axis_index("dp")
    x, z = lat_id % 4, lat_id // 4
    ylo, c = lyr // 2, lyr % 2
    y = h * 2 + ylo

    def at(xx=x, yy=y, zz=z, cc=c):
        return (zz * 4 + xx, (yy % 2) * 2 + cc, yy // 2)

    xp = [(x + o) % 4 for o in range(4)]
    yp = [(y + o) % 4 for o in range(4)]
    z_way = [at(zz=(z + 1) % 8), at(zz=(z + 7) % 8)]
    sibling = at(cc=1 - c)
    partner = at(yy=yp[2])
    remote = Copies()

    my_block = aligned((y * 2 + c) * 128, 128)
    my_cols = aligned(x * FB, FB)
    own = aligned((ylo * 2 + c) * 128, 128)
    x_cols = aligned(x * PIECE, PIECE)
    row0 = aligned((z % 4) * 128, 128)

    w_copy = pltpu.make_async_copy(w_hbm, w, local_sem.at[0])
    w_copy.start()
    own_copies = [
        pltpu.make_async_copy(
            lat.at[pl.ds(own, 128), :], la.at[pl.ds(my_block, 128), pl.ds(my_cols, FB)], local_sem.at[1]
        )
    ]
    for k in range(2):
        own_copies.append(
            pltpu.make_async_copy(
                w_hbm.at[:, pl.ds(aligned(k * HALF + x * PIECE, PIECE), PIECE)],
                wx.at[k, pl.ds(my_cols, FB), :],
                local_sem.at[2 + k],
            )
        )
    code_parts = []
    for k in range(2):
        ours = aligned(h * WIDTH + k * HALF + x * PIECE, PIECE)
        code_parts.append(
            pltpu.make_async_copy(
                codes.at[pl.ds(row0, 128), pl.ds(ours, PIECE)], mine_codes.at[k], local_sem.at[4 + k]
            )
        )
    for cp in own_copies + code_parts:
        cp.start()

    barrier = pltpu.get_barrier_semaphore()
    neighbours = [at(xx=xp[o]) for o in (1, 2, 3)] + [at(yy=yp[o]) for o in (1, 2, 3)]
    neighbours += [z_way[0], z_way[1], sibling]
    for d in neighbours:
        pl.semaphore_signal(barrier, inc=1, device_id=d, device_id_type=MESH)
    pl.semaphore_wait(barrier, len(neighbours))

    l1 = [
        remote.start(
            lat.at[pl.ds(own, 128), :],
            la.at[pl.ds(my_block, 128), pl.ds(my_cols, FB)],
            (l1a, l1b), o - 1, at(xx=xp[o]),
        )
        for o in (1, 2, 3)
    ]
    weights = [
        [
            remote.start(
                w_hbm.at[:, pl.ds(aligned(k * HALF + xp[o] * PIECE, PIECE), PIECE)],
                wx.at[k, pl.ds(my_cols, FB), :],
                (wa, wb), (k, o - 1), at(xx=xp[o]),
            )
            for o in (1, 2, 3)
        ]
        for k in range(2)
    ]
    misc = []
    for k in range(2):
        theirs = aligned((1 - h) * WIDTH + k * HALF + x * PIECE, PIECE)
        misc.append(
            remote.start(
                codes.at[pl.ds(row0, 128), pl.ds(theirs, PIECE)], other_codes.at[k], (ma, mb), k, partner
            )
        )
    misc.append(remote.start(sc.at[pl.ds(aligned((1 - h) * 16, 16), 16), :], sc_other, (ma, mb), 2, partner))

    for cp in own_copies:
        cp.wait()
    for cp in l1:
        cp.wait_recv()
    block = la.at[pl.ds(my_block, 128), :]
    l2 = {o: remote.start(block, block, (l2a, l2b), o - 1, at(yy=yp[o])) for o in (2, 1, 3)}
    l3 = [remote.start(block, block, (l3a, l3b), 0, sibling)]

    w_copy.wait()
    ones = jnp.ones((8, WIDTH), bf16)

    @pl.loop(0, 4)
    def _(i):
        at_f = aligned(i * 128, 128)
        wide = w[pl.ds(at_f, 128), :].astype(f32)
        square = wide * wide
        high = square.astype(bf16)
        low = (square - high.astype(f32)).astype(bf16)
        sq_mine[:, pl.ds(at_f, 128)] = lax.dot_general(
            ones, high, NT, preferred_element_type=f32
        ) + lax.dot_general(ones, low, NT, preferred_element_type=f32)

    misc.append(remote.start(sq_mine, sq_other, (ma, mb), 3, partner))

    def dots(chunk, k):
        rows = aligned(chunk * 256, 256)
        part[k, pl.ds(rows, 256), :] = jnp.dot(
            la[pl.ds(rows, 256), :], wx[k], preferred_element_type=f32
        )

    def pass_on(o, index):
        l2[o].wait_recv()
        arrived = la.at[pl.ds(aligned((yp[4 - o] * 2 + c) * 128, 128), 128), :]
        l3.append(remote.start(arrived, arrived, (l3a, l3b), index, sibling))

    for cp in weights[0]:
        cp.wait_recv()
    l3[0].wait_recv()
    dots(y, 0)
    pass_on(3, 1)
    pass_on(1, 2)
    l3[1].wait_recv()
    dots(yp[1], 0)
    pass_on(2, 3)
    l3[2].wait_recv()
    dots(yp[3], 0)
    l3[3].wait_recv()
    dots(yp[2], 0)

    def local_part(k, s, u, owner):
        return pl.ds(aligned(owner * 128 + s * 64 + u * 32, 32), 32)

    def ring_owner(s, step):
        return (z + 15 - step) % 8 if s == 0 else (z + 1 + step) % 8

    streams = [(s, u) for u in range(2) for s in range(2)]
    ring = {}

    def ring_start(k):
        for s, u in streams:
            ring[k, s, u] = remote.start(
                part.at[k, local_part(k, s, u, ring_owner(s, 0)), :],
                rs.at[k, s, u, 0], (rsa, rsb), (k, s, u, 0), z_way[s],
            )

    ring_start(0)
    for cp in weights[1]:
        cp.wait_recv()

    @pl.loop(0, 4)
    def _(i):
        dots(i, 1)

    ring_start(1)
    theirs = aligned((1 - h) * WIDTH, WIDTH)
    code_copies = [
        remote.start(
            codes.at[pl.ds(i * 128, 128), pl.ds(theirs, WIDTH)],
            codes_o.at[pl.ds(i * 128, 128), :],
            (ca, cb), i, partner,
        )
        for i in range(4)
    ]

    for step in range(1, 7):
        for k in range(2):
            for s, u in streams:
                ring[k, s, u].wait_recv()
                rs[k, s, u, step - 1] += part[k, local_part(k, s, u, ring_owner(s, step)), :]
                ring[k, s, u] = remote.start(
                    rs.at[k, s, u, step - 1], rs.at[k, s, u, step],
                    (rsa, rsb), (k, s, u, step), z_way[s],
                )

    for cp in code_parts:
        cp.wait()
    for cp in misc:
        cp.wait_recv()
    is_own = (z // 4) == h
    my_scales = jnp.where(
        is_own,
        sc[pl.ds(aligned(h * 16, 16), 16), pl.ds(row0, 128)].astype(f32),
        sc_other[:, pl.ds(row0, 128)].astype(f32),
    ).astype(bf16)
    squares = sq_mine[0:1, :] + sq_other[0:1, :]
    sq_o[...] = jnp.broadcast_to(squares, sq_o.shape)
    half_norms = (0.5 * penalty) * jnp.sqrt(squares + epsilon)
    sc_o[...] = sc_other[...]
    z_rows = aligned(z * 128, 128)

    def residual(k):
        wide_codes = jnp.where(is_own, mine_codes[k].astype(f32), other_codes[k].astype(f32))
        inputs = wide_codes * spread(my_scales, k * 8 + x * 2, PIECE)
        shift = bias[:, pl.ds(aligned(h * WIDTH + k * HALF + x * PIECE, PIECE), PIECE)]
        for s, u in streams:
            ring[k, s, u].wait_recv()
            recon = rs[k, s, u, 6] + part[k, local_part(k, s, u, z), :]
            first = s * 64 + u * 32
            value = (recon + shift - inputs[first : first + 32, :]).astype(bf16)
            resid[k, pl.ds(aligned(z * 128 + first, 32), 32), pl.ds(x_cols, PIECE)] = value

    def send_x(k, owner, sems, index):
        tile = resid.at[k, pl.ds(aligned(owner * 128, 128), 128), pl.ds(x_cols, PIECE)]
        return [
            remote.start(tile, tile, sems, (index, o - 1), at(xx=xp[o])) for o in (2, 1, 3)
        ]

    def block_at(way, distance):
        return (z + 8 - distance) % 8 if way == 0 else (z + distance) % 8

    zc = {}

    def send_z(k, way, j):
        sub = j % 2 if way == 0 else 1 - j % 2
        rows = pl.ds(aligned(block_at(way, j // 2) * 128 + sub * 64, 64), 64)
        cols = pl.ds(0, HALF) if k == 0 else pl.ds(x_cols, PIECE)
        tile = resid.at[k, rows, cols]
        sems = (z0a, z0b) if k == 0 else (z1a, z1b)
        zc[k, way, j] = remote.start(tile, tile, sems, (way, j), z_way[way])

    residual(0)
    x0 = send_x(0, z, (x0a, x0b), 0)
    residual(1)
    for way in range(2):
        for j in range(2):
            send_z(1, way, j)
    order = [z, block_at(0, 1), block_at(1, 1), block_at(0, 2), block_at(1, 2), block_at(0, 3), block_at(1, 3)]
    order.append((z + 4) % 8)
    x1 = [send_x(1, z, (x1a, x1b), 0)]
    for cp in x0:
        cp.wait_recv()
    for j in range(2):
        for way in range(2):
            send_z(0, way, j)
    for j in range(7):
        for way in range(2):
            zc[1, way, j].wait_recv()
            if j + 2 < 7:
                send_z(1, way, j + 2)
            if j % 2 == 1:
                x1.append(send_x(1, order[len(x1)], (x1a, x1b), len(x1)))
    x1.append(send_x(1, order[7], (x1a, x1b), 7))

    core_rows = aligned(c * 64, 64)
    y_rows = aligned(y * 16, 16)
    gc, gy, py, pc = {}, {}, {}, {}

    def first(i):
        for cp in x1[i]:
            cp.wait_recv()
        start = order[i] * 128
        rows = pl.ds(aligned(start, 128), 128)
        grad[i] = (
            lax.dot_general(resid[0, rows, :], w[:, :HALF], NT, preferred_element_type=f32)
            + lax.dot_general(resid[1, rows, :], w[:, HALF:], NT, preferred_element_type=f32)
            + half_norms
        )
        theirs = pl.ds(aligned((1 - c) * 64, 64), 64)
        gc[i] = remote.start(grad.at[i, theirs, :], core_in.at[i], (gca, gcb), i, sibling)

    def second(i):
        gc[i].wait_recv()
        core_sum[i] = core_in[i] + grad[i, pl.ds(core_rows, 64), :]
        gy[i] = [
            remote.start(
                core_sum.at[i, pl.ds(aligned(yp[o] * 16, 16), 16), :], y_in.at[i, o - 1],
                (gya, gyb), (i, o - 1), at(yy=yp[o]),
            )
            for o in (2, 1, 3)
        ]

    def third(i):
        for cp in gy[i]:
            cp.wait_recv()
        total = core_sum[i, pl.ds(y_rows, 16), :] + y_in[i, 0] + y_in[i, 1] + y_in[i, 2]
        rows = pl.ds(aligned(order[i] * 128 + c * 64 + y * 16, 16), 16)
        active = la[rows, pl.ds(my_cols, FB)].astype(f32) > 0
        pre[rows, :] = jnp.where(active, total, 0.0).astype(bf16)
        tile = pre.at[rows, :]
        py[i] = [remote.start(tile, tile, (pya, pyb), (i, o - 1), at(yy=yp[o])) for o in (2, 1, 3)]

    def fourth(i):
        for cp in py[i]:
            cp.wait_recv()
        tile = pre.at[pl.ds(aligned(order[i] * 128 + c * 64, 64), 64), :]
        pc[i] = remote.start(tile, tile, (pca, pcb), i, sibling)

    def stages(t):
        for lag, stage in enumerate((first, second, third, fourth)):
            if 0 <= t - lag < 8:
                stage(t - lag)

    stages(0)
    for j in range(7):
        for way in range(2):
            zc[0, way, j].wait_recv()
            if j + 2 < 7:
                send_z(0, way, j + 2)
            if j % 2 == 1:
                stages(j + way)
    out_copies = [
        pltpu.make_async_copy(resid, resid_o, local_sem.at[6]),
        pltpu.make_async_copy(la.at[:, pl.ds(my_cols, FB)], acts_o, local_sem.at[7]),
    ]
    stages(7)
    for cp in out_copies:
        cp.start()
    for t in range(8, 11):
        stages(t)
    for cp in pc.values():
        cp.wait_recv()
    pre_o[...] = pre[...]
    for cp in code_copies:
        cp.wait_recv()
    for cp in out_copies:
        cp.wait()
    remote.finish()


def exchange(lat, w, sc, bias, codes):
    vmem = pl.BlockSpec(memory_space=pltpu.VMEM)
    hbm = pl.BlockSpec(memory_space=pl.ANY)
    shape = jax.ShapeDtypeStruct
    pairs = [(3,), (2, 3), (3,), (4,), (2, 2, 2, 7), (1, 3), (2, 7), (2, 7), (8, 3), (8,), (8, 3), (8, 3), (8,), (4,), (4,)]
    return pl.pallas_call(
        exchange_kernel,
        out_shape=[
            shape((2, ROWS, HALF), bf16),
            shape((ROWS, FB), bf16),
            shape((ROWS, FB), bf16),
            shape((8, FB), f32),
            shape((ROWS // 2, WIDTH), bf16),
            shape((16, ROWS // 2), bf16),
        ],
        in_specs=[hbm, hbm, vmem, vmem, hbm],
        out_specs=[hbm, hbm, vmem, vmem, hbm, vmem],
        scratch_shapes=[
            pltpu.VMEM((ROWS, 4 * FB), bf16),
            pltpu.VMEM((FB, WIDTH), bf16),
            pltpu.VMEM((2, 4 * FB, PIECE), bf16),
            pltpu.VMEM((2, ROWS, PIECE), f32),
            pltpu.VMEM((2, 2, 2, 7, 32, PIECE), f32),
            pltpu.VMEM((2, ROWS, HALF), bf16),
            pltpu.VMEM((8, 128, FB), f32),
            pltpu.VMEM((8, 64, FB), f32),
            pltpu.VMEM((8, 64, FB), f32),
            pltpu.VMEM((8, 3, 16, FB), f32),
            pltpu.VMEM((ROWS, FB), bf16),
            pltpu.VMEM((2, 128, PIECE), bf16),
            pltpu.VMEM((2, 128, PIECE), bf16),
            pltpu.VMEM((8, FB), f32),
            pltpu.VMEM((8, FB), f32),
            pltpu.VMEM((16, ROWS // 2), bf16),
            pltpu.SemaphoreType.DMA((8,)),
        ]
        + [pltpu.SemaphoreType.DMA(count) for count in pairs for _ in range(2)],
        compiler_params=pltpu.CompilerParams(
            collective_id=0, has_side_effects=True, vmem_limit_bytes=50 * 2**20
        ),
        name="exchange",
    )(lat, w, sc, bias, codes)


def grads_kernel(half, acts, resid, w, pre, squares, own_codes, other_codes, own_sc, other_sc, enc_o, dec_o, bias_o):
    step = pl.program_id(0)
    h = half[0]
    act_sum = jnp.sum(acts[...].astype(f32), axis=0, keepdims=True)
    scale = penalty * act_sum / jnp.sqrt(squares[0:1, :] + epsilon)
    column = jnp.broadcast_to(scale, (128, 128)).T
    for k in range(2):
        term = lax.dot_general(acts[...], resid[k], TN, preferred_element_type=f32)
        for j in range(8):
            cols = slice(k * HALF + j * 128, k * HALF + j * 128 + 128)
            dec_o[pl.ds(k * 8 + j, 128, stride=16), :] = (
                term[:, j * 128 : j * 128 + 128] + column * w[:, cols].astype(f32)
            )
    own_at = pl.multiple_of(h * 512, 512)
    other_at = pl.multiple_of((1 - h) * 512, 512)
    own_in = (own_codes[...].astype(f32) * spread(own_sc[...], step * 4, 512)).astype(bf16)
    other_in = (other_codes[...].astype(f32) * spread(other_sc[...], step * 4, 512)).astype(bf16)
    enc = lax.dot_general(own_in, pre[pl.ds(own_at, 512), :], TN, preferred_element_type=f32)
    enc += lax.dot_general(other_in, pre[pl.ds(other_at, 512), :], TN, preferred_element_type=f32)
    for j in range(4):
        enc_o[pl.ds(j, 512, stride=4), :] = enc[:, j * 128 : j * 128 + 128]

    @pl.when(step == 0)
    def _():
        bias_o[...] = jnp.broadcast_to(jnp.sum(pre[...].astype(f32), axis=0, keepdims=True), bias_o.shape)


def grads(half, acts, resid, w, pre, squares, codes, other_codes, sc, other_sc):
    whole = lambda *shape: pl.BlockSpec(shape, lambda i, h: (0,) * len(shape))
    return pl.pallas_call(
        grads_kernel,
        grid_spec=pltpu.PrefetchScalarGridSpec(
            num_scalar_prefetch=1,
            grid=(4,),
            in_specs=[
                pl.BlockSpec((ROWS, 128), lambda i, h: (0, i)),
                whole(2, ROWS, HALF),
                pl.BlockSpec((128, WIDTH), lambda i, h: (i, 0)),
                whole(ROWS, FB),
                pl.BlockSpec((8, 128), lambda i, h: (0, i)),
                pl.BlockSpec((512, 512), lambda i, h: (0, h[0] * 4 + i)),
                pl.BlockSpec((512, 512), lambda i, h: (0, i)),
                pl.BlockSpec((16, 512), lambda i, h: (h[0], 0)),
                whole(16, 512),
            ],
            out_specs=[
                pl.BlockSpec((2048, 128), lambda i, h: (i, 0)),
                pl.BlockSpec((2048, 128), lambda i, h: (i, 0)),
                whole(8, FB),
            ],
        ),
        out_shape=[
            jax.ShapeDtypeStruct((WIDTH * 4, 128), f32),
            jax.ShapeDtypeStruct((FB * 16, 128), f32),
            jax.ShapeDtypeStruct((8, FB), f32),
        ],
        compiler_params=pltpu.CompilerParams(vmem_limit_bytes=50 * 2**20),
        name="grads",
    )(half, acts, resid, w, pre, squares, codes, other_codes, sc, other_sc)


def shards(act_codes, act_scales, latents, dec_weight, dec_bias):
    w = dec_weight[:, 0, :]
    codes = act_codes[:, 0, :]
    sc = act_scales[:, 0, :].T
    resid, acts, pre, squares, other_codes, other_sc = exchange(latents, w, sc, dec_bias, codes)
    half = lax.axis_index("dp").astype(jnp.int32).reshape(1)
    enc, dec, bias = grads(half, acts, resid, w, pre, squares, codes, other_codes, sc, other_sc)
    return enc.reshape(WIDTH, 1, FB), dec.reshape(FB, 1, WIDTH), bias[0]


def solution(mesh):
    in_specs = (
        P("dp", "lyr", None),
        P("dp", "lyr", None),
        P("dp", "lat"),
        P("lat", "lyr", "dp"),
        P("lyr", None),
    )
    out_specs = (P("dp", "lyr", "lat"), P("lat", "lyr", "dp"), P("lat"))
    return jax.shard_map(shards, mesh=mesh, in_specs=in_specs, out_specs=out_specs, check_vma=False)
```

```python
import functools

import jax
import jax.numpy as jnp
from jax import lax
from jax.experimental import pallas as pl
from jax.experimental.pallas import tpu as pltpu
from jax.sharding import PartitionSpec as P

penalty = 1.0
epsilon = 1e-06
MESH = pl.DeviceIdType.MESH
f32, bf16 = jnp.float32, jnp.bfloat16

ROWS, FB, WIDTH = 1024, 512, 2048
HALF = WIDTH // 2
PIECE = HALF // 4
LAG = 0
VMEM_LIMIT = 56 * 2**20
NT = (((1,), (1,)), ((), ()))
TN = (((0,), (0,)), ((), ()))


def aligned(value, step):
    return pl.multiple_of(value, step)


def spread(scales, first, width):
    blocks = scales.shape[0]
    row = lax.broadcasted_iota(jnp.int32, (blocks, width), 0)
    col = lax.broadcasted_iota(jnp.int32, (blocks, width), 1)
    pick = jnp.where(row == first + col // 128, 1.0, 0.0).astype(bf16)
    return lax.dot_general(scales, pick, TN, preferred_element_type=f32)


class Copies:
    def __init__(self):
        self.started = []

    def start(self, src, dst, sems, index, device):
        cp = pltpu.make_async_remote_copy(
            src_ref=src,
            dst_ref=dst,
            send_sem=sems[0].at[index],
            recv_sem=sems[1].at[index],
            device_id=device,
            device_id_type=MESH,
        )
        cp.start()
        self.started.append(cp)
        return cp

    def finish(self):
        for cp in self.started:
            cp.wait_send()


def exchange_kernel(
    lat, w_hbm, sc, bias, codes,
    resid_o, acts_o, pre_o, sq_o, in_o,
    la, w, wx, part, rs, resid, grad, core_in, core_sum, y_in, pre, mine_codes, other_codes, sq_mine, sq_other, sc_other, codes_v, sc_wide, turned, w_t,
    local_sem,
    l1a, l1b, wa, wb, l2a, l2b, l3a, l3b, rsa, rsb, x0a, x0b, z0a, z0b, z1a, z1b, x1a, x1b,
    gca, gcb, gya, gyb, pya, pyb, pca, pcb, ma, mb, ca, cb,
):
    lat_id = lax.axis_index("lat")
    lyr = lax.axis_index("lyr")
    h = lax.axis_index("dp")
    x, z = lat_id % 4, lat_id // 4
    ylo, c = lyr // 2, lyr % 2
    y = h * 2 + ylo

    def at(xx=x, yy=y, zz=z, cc=c):
        return (zz * 4 + xx, (yy % 2) * 2 + cc, yy // 2)

    xp = [(x + o) % 4 for o in range(4)]
    yp = [(y + o) % 4 for o in range(4)]
    z_way = [at(zz=(z + 1) % 8), at(zz=(z + 7) % 8)]
    sibling = at(cc=1 - c)
    partner = at(yy=yp[2])
    remote = Copies()

    my_block = aligned((y * 2 + c) * 128, 128)
    my_cols = aligned(x * FB, FB)
    own = aligned((ylo * 2 + c) * 128, 128)
    x_cols = aligned(x * PIECE, PIECE)
    row0 = aligned((z % 4) * 128, 128)

    w_copy = pltpu.make_async_copy(w_hbm, w, local_sem.at[0])
    w_copy.start()
    own_copies = [
        pltpu.make_async_copy(
            lat.at[pl.ds(own, 128), :], la.at[pl.ds(my_block, 128), pl.ds(my_cols, FB)], local_sem.at[1]
        )
    ]
    for k in range(2):
        own_copies.append(
            pltpu.make_async_copy(
                w_hbm.at[:, pl.ds(aligned(k * HALF + x * PIECE, PIECE), PIECE)],
                wx.at[k, pl.ds(my_cols, FB), :],
                local_sem.at[2 + k],
            )
        )
    codes_copy = pltpu.make_async_copy(codes, codes_v, local_sem.at[8])
    code_parts = []
    for k in range(2):
        ours = aligned(h * WIDTH + k * HALF + x * PIECE, PIECE)
        code_parts.append(
            pltpu.make_async_copy(
                codes.at[pl.ds(row0, 128), pl.ds(ours, PIECE)], mine_codes.at[k], local_sem.at[4 + k]
            )
        )
    for cp in own_copies + code_parts + [codes_copy]:
        cp.start()

    barrier = pltpu.get_barrier_semaphore()
    neighbours = [at(xx=xp[o]) for o in (1, 2, 3)] + [at(yy=yp[o]) for o in (1, 2, 3)]
    neighbours += [z_way[0], z_way[1], sibling]
    for d in neighbours:
        pl.semaphore_signal(barrier, inc=1, device_id=d, device_id_type=MESH)
    pl.semaphore_wait(barrier, len(neighbours))

    l1 = [
        remote.start(
            lat.at[pl.ds(own, 128), :],
            la.at[pl.ds(my_block, 128), pl.ds(my_cols, FB)],
            (l1a, l1b), o - 1, at(xx=xp[o]),
        )
        for o in (1, 2, 3)
    ]
    misc = []
    for k in range(2):
        theirs = aligned((1 - h) * WIDTH + k * HALF + x * PIECE, PIECE)
        misc.append(
            remote.start(
                codes.at[pl.ds(row0, 128), pl.ds(theirs, PIECE)], other_codes.at[k], (ma, mb), k, partner
            )
        )
    misc.append(remote.start(sc.at[pl.ds(aligned((1 - h) * 16, 16), 16), :], sc_other, (ma, mb), 2, partner))

    for cp in own_copies:
        cp.wait()
    for cp in l1:
        cp.wait_recv()
    block = la.at[pl.ds(my_block, 128), :]
    l2 = {o: remote.start(block, block, (l2a, l2b), o - 1, at(yy=yp[o])) for o in (1, 3)}
    weights = [
        [
            remote.start(
                w_hbm.at[:, pl.ds(aligned(k * HALF + xp[o] * PIECE, PIECE), PIECE)],
                wx.at[k, pl.ds(my_cols, FB), :],
                (wa, wb), (k, o - 1), at(xx=xp[o]),
            )
            for o in (1, 2, 3)
        ]
        for k in range(2)
    ]
    l3 = [remote.start(block, block, (l3a, l3b), 0, sibling)]

    w_copy.wait()
    ones = jnp.ones((8, WIDTH), bf16)

    @pl.loop(0, 4)
    def _(i):
        at_f = aligned(i * 128, 128)
        wide = w[pl.ds(at_f, 128), :].astype(f32)
        square = wide * wide
        high = square.astype(bf16)
        low = (square - high.astype(f32)).astype(bf16)
        sq_mine[:, pl.ds(at_f, 128)] = lax.dot_general(
            ones, high, NT, preferred_element_type=f32
        ) + lax.dot_general(ones, low, NT, preferred_element_type=f32)

    misc.append(remote.start(sq_mine, sq_other, (ma, mb), 3, partner))

    def turn_weights(i, carry):
        cols = pl.ds(aligned(i * 128, 128), 128)
        w_t[cols, :] = w[:, cols].astype(f32).T.astype(bf16)
        return carry

    lax.fori_loop(0, 16, turn_weights, 0)

    def dots(chunk, k):
        rows = aligned(chunk * 256, 256)
        part[k, pl.ds(rows, 256), :] = jnp.dot(
            la[pl.ds(rows, 256), :], wx[k], preferred_element_type=f32
        )

    codes_copy.wait()
    sc_wide[...] = sc[...].astype(f32)

    def turn(i, carry):
        cols = pl.ds(aligned(i * 128, 128), 128)
        turned[cols, :] = (codes_v[:, cols].astype(f32).T * sc_wide[pl.ds(i, 1), :]).astype(bf16)
        return carry

    lax.fori_loop(0, 16, turn, 0)

    def rows_of(yy, cc, part_of=0, parts=1):
        count = 128 // parts
        return la.at[pl.ds(aligned((yy * 2 + cc) * 128 + part_of * count, count), count), :]

    for o in (1, 3):
        l2[o].wait_recv()
        arrived = rows_of(yp[4 - o], c)
        l3.append(remote.start(arrived, arrived, (l3a, l3b), o, sibling))
        half = rows_of(yp[4 - o], c, 0 if o == 1 else 1, 2)
        l2[o, 2] = remote.start(half, half, (l2a, l2b), 1 if o == 1 else 3, at(yy=yp[o]))

    lax.fori_loop(16, 32, turn, 0)
    for o in (1, 3):
        l2[o, 2].wait_recv()
    arrived = rows_of(yp[2], c)
    l3.append(remote.start(arrived, arrived, (l3a, l3b), 2, sibling))

    for cp in weights[0] + l3:
        cp.wait_recv()

    @pl.loop(0, 4)
    def _(i):
        dots(i, 0)

    def local_part(k, s, u, owner):
        return pl.ds(aligned(owner * 128 + s * 64 + u * 32, 32), 32)

    def ring_owner(s, step):
        return (z + 15 - step) % 8 if s == 0 else (z + 1 + step) % 8

    streams = [(s, u) for u in range(2) for s in range(2)]
    ring = {}

    def ring_start(k):
        for s, u in streams:
            ring[k, s, u] = remote.start(
                part.at[k, local_part(k, s, u, ring_owner(s, 0)), :],
                rs.at[k, s, u, 0], (rsa, rsb), (k, s, u, 0), z_way[s],
            )

    ring_start(0)
    for cp in weights[1]:
        cp.wait_recv()

    @pl.loop(0, 4)
    def _(i):
        dots(i, 1)

    ring_start(1)
    in_copies = [
        pltpu.make_async_copy(
            turned.at[pl.ds(aligned(h * WIDTH, WIDTH), WIDTH), :],
            in_o.at[h],
            local_sem.at[9],
        )
    ]
    in_copies[0].start()
    in_sends = [
        remote.start(
            turned.at[pl.ds(aligned((1 - h) * WIDTH + i * 512, 512), 512), :],
            in_o.at[h, pl.ds(i * 512, 512), :],
            (ca, cb), i, partner,
        )
        for i in range(4)
    ]
    for step in range(1, 7):
        for k in range(2):
            for s, u in streams:
                ring[k, s, u].wait_recv()
                rs[k, s, u, step - 1] += part[k, local_part(k, s, u, ring_owner(s, step)), :]
                ring[k, s, u] = remote.start(
                    rs.at[k, s, u, step - 1], rs.at[k, s, u, step],
                    (rsa, rsb), (k, s, u, step), z_way[s],
                )

    for cp in code_parts:
        cp.wait()
    for cp in misc:
        cp.wait_recv()
    is_own = (z // 4) == h
    my_scales = jnp.where(
        is_own,
        sc[pl.ds(aligned(h * 16, 16), 16), pl.ds(row0, 128)].astype(f32),
        sc_other[:, pl.ds(row0, 128)].astype(f32),
    ).astype(bf16)
    squares = sq_mine[0:1, :] + sq_other[0:1, :]
    sq_o[...] = jnp.broadcast_to(squares, sq_o.shape)
    half_norms = (0.5 * penalty) * jnp.sqrt(squares + epsilon)
    z_rows = aligned(z * 128, 128)

    def residual(k):
        wide_codes = jnp.where(is_own, mine_codes[k].astype(f32), other_codes[k].astype(f32))
        inputs = wide_codes * spread(my_scales, k * 8 + x * 2, PIECE)
        shift = bias[:, pl.ds(aligned(h * WIDTH + k * HALF + x * PIECE, PIECE), PIECE)]
        for s, u in streams:
            ring[k, s, u].wait_recv()
            recon = rs[k, s, u, 6] + part[k, local_part(k, s, u, z), :]
            first = s * 64 + u * 32
            value = (recon + shift - inputs[first : first + 32, :]).astype(bf16)
            resid[k, pl.ds(aligned(z * 128 + first, 32), 32), pl.ds(x_cols, PIECE)] = value

    def send_x(k, owner, sems, index):
        tile = resid.at[k, pl.ds(aligned(owner * 128, 128), 128), pl.ds(x_cols, PIECE)]
        return [
            remote.start(tile, tile, sems, (index, o - 1), at(xx=xp[o])) for o in (2, 1, 3)
        ]

    def block_at(way, distance):
        return (z + 8 - distance) % 8 if way == 0 else (z + distance) % 8

    zc = {}

    def send_z(k, way, j):
        sub = j % 2 if way == 0 else 1 - j % 2
        rows = pl.ds(aligned(block_at(way, j // 2) * 128 + sub * 64, 64), 64)
        cols = pl.ds(0, HALF) if k == 0 else pl.ds(x_cols, PIECE)
        tile = resid.at[k, rows, cols]
        sems = (z0a, z0b) if k == 0 else (z1a, z1b)
        zc[k, way, j] = remote.start(tile, tile, sems, (way, j), z_way[way])

    residual(0)
    x0 = send_x(0, z, (x0a, x0b), 0)
    residual(1)
    for way in range(2):
        for j in range(2):
            send_z(1, way, j)
    order = [z, block_at(0, 1), block_at(1, 1), block_at(0, 2), block_at(1, 2), block_at(0, 3), block_at(1, 3)]
    order.append((z + 4) % 8)
    x1 = [send_x(1, z, (x1a, x1b), 0)]
    for cp in x0:
        cp.wait_recv()
    for j in range(2):
        for way in range(2):
            send_z(0, way, j)
    for j in range(7):
        for way in range(2):
            zc[1, way, j].wait_recv()
            if j + 2 < 7:
                send_z(1, way, j + 2)
            if j % 2 == 1:
                x1.append(send_x(1, order[len(x1)], (x1a, x1b), len(x1)))
    x1.append(send_x(1, order[7], (x1a, x1b), 7))

    core_rows = aligned(c * 64, 64)
    y_rows = aligned(y * 16, 16)
    gc, gy, py, pc = {}, {}, {}, {}

    def first(i):
        for cp in x1[i]:
            cp.wait_recv()
        start = order[i] * 128
        rows = pl.ds(aligned(start, 128), 128)
        grad[i] = (
            jnp.dot(resid[0, rows, :], w_t[:HALF, :], preferred_element_type=f32)
            + jnp.dot(resid[1, rows, :], w_t[HALF:, :], preferred_element_type=f32)
            + half_norms
        )
        theirs = pl.ds(aligned((1 - c) * 64, 64), 64)
        gc[i] = remote.start(grad.at[i, theirs, :], core_in.at[i], (gca, gcb), i, sibling)

    def second(i):
        gc[i].wait_recv()
        core_sum[i] = core_in[i] + grad[i, pl.ds(core_rows, 64), :]
        gy[i] = [
            remote.start(
                core_sum.at[i, pl.ds(aligned(yp[o] * 16, 16), 16), :], y_in.at[i, o - 1],
                (gya, gyb), (i, o - 1), at(yy=yp[o]),
            )
            for o in (2, 1, 3)
        ]

    def third(i):
        for cp in gy[i]:
            cp.wait_recv()
        total = core_sum[i, pl.ds(y_rows, 16), :] + y_in[i, 0] + y_in[i, 1] + y_in[i, 2]
        rows = pl.ds(aligned(order[i] * 128 + c * 64 + y * 16, 16), 16)
        active = la[rows, pl.ds(my_cols, FB)].astype(f32) > 0
        pre[rows, :] = jnp.where(active, total, 0.0).astype(bf16)
        tile = pre.at[rows, :]
        py[i] = [remote.start(tile, tile, (pya, pyb), (i, o - 1), at(yy=yp[o])) for o in (2, 1, 3)]

    def fourth(i):
        for cp in py[i]:
            cp.wait_recv()
        tile = pre.at[pl.ds(aligned(order[i] * 128 + c * 64, 64), 64), :]
        pc[i] = remote.start(tile, tile, (pca, pcb), i, sibling)

    def stages(t):
        for lag, stage in enumerate((first, second, third, fourth)):
            if 0 <= t - lag < 8:
                stage(t - lag)

    for j in range(7):
        for way in range(2):
            zc[0, way, j].wait_recv()
            if j + 2 < 7:
                send_z(0, way, j + 2)
        if j >= LAG:
            stages(j - LAG)
    out_copies = [
        pltpu.make_async_copy(resid, resid_o, local_sem.at[6]),
        pltpu.make_async_copy(la.at[:, pl.ds(my_cols, FB)], acts_o, local_sem.at[7]),
    ]
    for t in range(7 - LAG, 11):
        stages(t)
        if t == 7:
            for cp in out_copies:
                cp.start()
    for cp in pc.values():
        cp.wait_recv()
    pre_o[...] = pre[...]
    for cp in in_sends:
        cp.wait_recv()
    for cp in out_copies + in_copies:
        cp.wait()
    remote.finish()


def exchange(lat, w, sc, bias, codes):
    vmem = pl.BlockSpec(memory_space=pltpu.VMEM)
    hbm = pl.BlockSpec(memory_space=pl.ANY)
    shape = jax.ShapeDtypeStruct
    pairs = [(3,), (2, 3), (4,), (4,), (2, 2, 2, 7), (1, 3), (2, 7), (2, 7), (8, 3), (8,), (8, 3), (8, 3), (8,), (4,), (4,)]
    return pl.pallas_call(
        exchange_kernel,
        out_shape=[
            shape((2, ROWS, HALF), bf16),
            shape((ROWS, FB), bf16),
            shape((ROWS, FB), bf16),
            shape((8, FB), f32),
            shape((2, WIDTH, ROWS // 2), bf16),
        ],
        in_specs=[hbm, hbm, vmem, vmem, hbm],
        out_specs=[hbm, hbm, vmem, vmem, hbm],
        scratch_shapes=[
            pltpu.VMEM((ROWS, 4 * FB), bf16),
            pltpu.VMEM((FB, WIDTH), bf16),
            pltpu.VMEM((2, 4 * FB, PIECE), bf16),
            pltpu.VMEM((2, ROWS, PIECE), f32),
            pltpu.VMEM((2, 2, 2, 7, 32, PIECE), f32),
            pltpu.VMEM((2, ROWS, HALF), bf16),
            pltpu.VMEM((8, 128, FB), f32),
            pltpu.VMEM((8, 64, FB), f32),
            pltpu.VMEM((8, 64, FB), f32),
            pltpu.VMEM((8, 3, 16, FB), f32),
            pltpu.VMEM((ROWS, FB), bf16),
            pltpu.VMEM((2, 128, PIECE), bf16),
            pltpu.VMEM((2, 128, PIECE), bf16),
            pltpu.VMEM((8, FB), f32),
            pltpu.VMEM((8, FB), f32),
            pltpu.VMEM((16, ROWS // 2), bf16),
            pltpu.VMEM((ROWS // 2, 2 * WIDTH), bf16),
            pltpu.VMEM((32, ROWS // 2), f32),
            pltpu.VMEM((2 * WIDTH, ROWS // 2), bf16),
            pltpu.VMEM((WIDTH, FB), bf16),
            pltpu.SemaphoreType.DMA((10,)),
        ]
        + [pltpu.SemaphoreType.DMA(count) for count in pairs for _ in range(2)],
        compiler_params=pltpu.CompilerParams(
            collective_id=0, has_side_effects=True, vmem_limit_bytes=VMEM_LIMIT
        ),
        name="exchange",
    )(lat, w, sc, bias, codes)


def grads_kernel(acts, resid, w, pre, squares, inputs, enc_o, dec_o, bias_o):
    act_sum = jnp.sum(acts[...].astype(f32), axis=0, keepdims=True)
    scale = penalty * act_sum / jnp.sqrt(squares[0:1, :] + epsilon)
    column = jnp.broadcast_to(scale, (128, 128)).T
    for k in range(2):
        term = lax.dot_general(acts[...], resid[k], TN, preferred_element_type=f32)
        for j in range(8):
            cols = slice(k * HALF + j * 128, k * HALF + j * 128 + 128)
            dec_o[pl.ds(k * 8 + j, 128, stride=16), :] = (
                term[:, j * 128 : j * 128 + 128] + column * w[:, cols].astype(f32)
            )
    enc = jnp.dot(inputs[0], pre[: ROWS // 2, :], preferred_element_type=f32)
    enc += jnp.dot(inputs[1], pre[ROWS // 2 :, :], preferred_element_type=f32)
    for j in range(4):
        enc_o[pl.ds(j, 512, stride=4), :] = enc[:, j * 128 : j * 128 + 128]

    @pl.when(pl.program_id(0) == 0)
    def _():
        bias_o[...] = jnp.sum(pre[...].astype(f32), axis=0, keepdims=True)


def grads(acts, resid, w, pre, squares, inputs):
    whole = lambda *shape: pl.BlockSpec(shape, lambda i: (0,) * len(shape))
    return pl.pallas_call(
        grads_kernel,
        grid=(4,),
        in_specs=[
            pl.BlockSpec((ROWS, 128), lambda i: (0, i)),
            whole(2, ROWS, HALF),
            pl.BlockSpec((128, WIDTH), lambda i: (i, 0)),
            whole(ROWS, FB),
            pl.BlockSpec((8, 128), lambda i: (0, i)),
            pl.BlockSpec((2, 512, ROWS // 2), lambda i: (0, i, 0)),
        ],
        out_specs=[
            pl.BlockSpec((2048, 128), lambda i: (i, 0)),
            pl.BlockSpec((2048, 128), lambda i: (i, 0)),
            whole(1, FB),
        ],
        out_shape=[
            jax.ShapeDtypeStruct((WIDTH * 4, 128), f32),
            jax.ShapeDtypeStruct((FB * 16, 128), f32),
            jax.ShapeDtypeStruct((1, FB), f32),
        ],
        compiler_params=pltpu.CompilerParams(vmem_limit_bytes=50 * 2**20),
        name="grads",
    )(acts, resid, w, pre, squares, inputs)


def shards(act_codes, act_scales, latents, dec_weight, dec_bias):
    w = dec_weight[:, 0, :]
    resid, acts, pre, squares, inputs = exchange(
        latents, w, act_scales[:, 0, :].T, dec_bias, act_codes[:, 0, :]
    )
    enc, dec, bias = grads(acts, resid, w, pre, squares, inputs)
    return enc.reshape(WIDTH, 1, FB), dec.reshape(FB, 1, WIDTH), bias.reshape(FB)


def solution(mesh):
    in_specs = (
        P("dp", "lyr", None),
        P("dp", "lyr", None),
        P("dp", "lat"),
        P("lat", "lyr", "dp"),
        P("lyr", None),
    )
    out_specs = (P("dp", "lyr", "lat"), P("lat", "lyr", "dp"), P("lat"))
    return jax.shard_map(shards, mesh=mesh, in_specs=in_specs, out_specs=out_specs, check_vma=False)
```

```python
import functools

import jax
import jax.numpy as jnp
from jax import lax
from jax.experimental import pallas as pl
from jax.experimental.pallas import tpu as pltpu
from jax.sharding import PartitionSpec as P

penalty = 1.0
epsilon = 1e-06
MESH = pl.DeviceIdType.MESH
f32, bf16 = jnp.float32, jnp.bfloat16

ROWS, FB, WIDTH = 1024, 512, 2048
HALF = WIDTH // 2
PIECE = HALF // 4
LAGS = (0, 1, 3, 5)
VMEM_LIMIT = 56 * 2**20
NT = (((1,), (1,)), ((), ()))
TN = (((0,), (0,)), ((), ()))


def aligned(value, step):
    return pl.multiple_of(value, step)


def spread(scales, first, width):
    blocks = scales.shape[0]
    row = lax.broadcasted_iota(jnp.int32, (blocks, width), 0)
    col = lax.broadcasted_iota(jnp.int32, (blocks, width), 1)
    pick = jnp.where(row == first + col // 128, 1.0, 0.0).astype(bf16)
    return lax.dot_general(scales, pick, TN, preferred_element_type=f32)


class Copies:
    def __init__(self):
        self.started = []

    def start(self, src, dst, sems, index, device):
        cp = pltpu.make_async_remote_copy(
            src_ref=src,
            dst_ref=dst,
            send_sem=sems[0].at[index],
            recv_sem=sems[1].at[index],
            device_id=device,
            device_id_type=MESH,
        )
        cp.start()
        self.started.append(cp)
        return cp

    def finish(self):
        for cp in self.started:
            cp.wait_send()


def exchange_kernel(
    lat, w_hbm, sc, bias, codes,
    resid_o, acts_o, pre_o, sq_o, in_o,
    la, w, wx, part, rs, resid, grad, core_in, core_sum, y_in, pre, mine_codes, other_codes, sq_mine, sq_other, sc_other, codes_v, sc_wide, turned, w_t,
    local_sem,
    l1a, l1b, wa, wb, l2a, l2b, l3a, l3b, rsa, rsb, x0a, x0b, z0a, z0b, z1a, z1b, x1a, x1b,
    gca, gcb, gya, gyb, pya, pyb, pca, pcb, ma, mb, ca, cb,
):
    lat_id = lax.axis_index("lat")
    lyr = lax.axis_index("lyr")
    h = lax.axis_index("dp")
    x, z = lat_id % 4, lat_id // 4
    ylo, c = lyr // 2, lyr % 2
    y = h * 2 + ylo

    def at(xx=x, yy=y, zz=z, cc=c):
        return (zz * 4 + xx, (yy % 2) * 2 + cc, yy // 2)

    xp = [(x + o) % 4 for o in range(4)]
    yp = [(y + o) % 4 for o in range(4)]
    z_way = [at(zz=(z + 1) % 8), at(zz=(z + 7) % 8)]
    sibling = at(cc=1 - c)
    partner = at(yy=yp[2])
    remote = Copies()

    my_block = aligned((y * 2 + c) * 128, 128)
    my_cols = aligned(x * FB, FB)
    own = aligned((ylo * 2 + c) * 128, 128)
    x_cols = aligned(x * PIECE, PIECE)
    row0 = aligned((z % 4) * 128, 128)

    w_copy = pltpu.make_async_copy(w_hbm, w, local_sem.at[0])
    w_copy.start()
    own_copies = [
        pltpu.make_async_copy(
            lat.at[pl.ds(own, 128), :], la.at[pl.ds(my_block, 128), pl.ds(my_cols, FB)], local_sem.at[1]
        )
    ]
    for k in range(2):
        own_copies.append(
            pltpu.make_async_copy(
                w_hbm.at[:, pl.ds(aligned(k * HALF + x * PIECE, PIECE), PIECE)],
                wx.at[k, pl.ds(my_cols, FB), :],
                local_sem.at[2 + k],
            )
        )
    codes_copy = pltpu.make_async_copy(codes, codes_v, local_sem.at[8])
    code_parts = []
    for k in range(2):
        ours = aligned(h * WIDTH + k * HALF + x * PIECE, PIECE)
        code_parts.append(
            pltpu.make_async_copy(
                codes.at[pl.ds(row0, 128), pl.ds(ours, PIECE)], mine_codes.at[k], local_sem.at[4 + k]
            )
        )
    for cp in own_copies + code_parts + [codes_copy]:
        cp.start()

    barrier = pltpu.get_barrier_semaphore()
    neighbours = [at(xx=xp[o]) for o in (1, 2, 3)] + [at(yy=yp[o]) for o in (1, 2, 3)]
    neighbours += [z_way[0], z_way[1], sibling]
    for d in neighbours:
        pl.semaphore_signal(barrier, inc=1, device_id=d, device_id_type=MESH)
    pl.semaphore_wait(barrier, len(neighbours))

    l1 = [
        remote.start(
            lat.at[pl.ds(own, 128), :],
            la.at[pl.ds(my_block, 128), pl.ds(my_cols, FB)],
            (l1a, l1b), o - 1, at(xx=xp[o]),
        )
        for o in (1, 2, 3)
    ]
    misc = []
    for k in range(2):
        theirs = aligned((1 - h) * WIDTH + k * HALF + x * PIECE, PIECE)
        misc.append(
            remote.start(
                codes.at[pl.ds(row0, 128), pl.ds(theirs, PIECE)], other_codes.at[k], (ma, mb), k, partner
            )
        )
    misc.append(remote.start(sc.at[pl.ds(aligned((1 - h) * 16, 16), 16), :], sc_other, (ma, mb), 2, partner))

    for cp in own_copies:
        cp.wait()
    for cp in l1:
        cp.wait_recv()
    block = la.at[pl.ds(my_block, 128), :]
    l2 = {o: remote.start(block, block, (l2a, l2b), o - 1, at(yy=yp[o])) for o in (1, 3)}
    weights = [
        [
            remote.start(
                w_hbm.at[:, pl.ds(aligned(k * HALF + xp[o] * PIECE, PIECE), PIECE)],
                wx.at[k, pl.ds(my_cols, FB), :],
                (wa, wb), (k, o - 1), at(xx=xp[o]),
            )
            for o in (1, 2, 3)
        ]
        for k in range(2)
    ]
    l3 = [remote.start(block, block, (l3a, l3b), 0, sibling)]

    w_copy.wait()
    ones = jnp.ones((8, WIDTH), bf16)

    @pl.loop(0, 4)
    def _(i):
        at_f = aligned(i * 128, 128)
        wide = w[pl.ds(at_f, 128), :].astype(f32)
        square = wide * wide
        high = square.astype(bf16)
        low = (square - high.astype(f32)).astype(bf16)
        sq_mine[:, pl.ds(at_f, 128)] = lax.dot_general(
            ones, high, NT, preferred_element_type=f32
        ) + lax.dot_general(ones, low, NT, preferred_element_type=f32)

    misc.append(remote.start(sq_mine, sq_other, (ma, mb), 3, partner))

    def turn_weights(i, carry):
        cols = pl.ds(aligned(i * 128, 128), 128)
        w_t[cols, :] = w[:, cols].astype(f32).T.astype(bf16)
        return carry

    lax.fori_loop(0, 16, turn_weights, 0)

    def dots(chunk, k):
        rows = aligned(chunk * 256, 256)
        part[k, pl.ds(rows, 256), :] = jnp.dot(
            la[pl.ds(rows, 256), :], wx[k], preferred_element_type=f32
        )

    codes_copy.wait()
    sc_wide[...] = sc[...].astype(f32)

    def turn(i, carry):
        cols = pl.ds(aligned(i * 128, 128), 128)
        turned[cols, :] = (codes_v[:, cols].astype(f32).T * sc_wide[pl.ds(i, 1), :]).astype(bf16)
        return carry

    lax.fori_loop(0, 16, turn, 0)

    def rows_of(yy, cc, part_of=0, parts=1):
        count = 128 // parts
        return la.at[pl.ds(aligned((yy * 2 + cc) * 128 + part_of * count, count), count), :]

    for o in (1, 3):
        l2[o].wait_recv()
        arrived = rows_of(yp[4 - o], c)
        l3.append(remote.start(arrived, arrived, (l3a, l3b), o, sibling))
        half = rows_of(yp[4 - o], c, 0 if o == 1 else 1, 2)
        l2[o, 2] = remote.start(half, half, (l2a, l2b), 1 if o == 1 else 3, at(yy=yp[o]))

    lax.fori_loop(16, 32, turn, 0)
    for o in (1, 3):
        l2[o, 2].wait_recv()
    arrived = rows_of(yp[2], c)
    l3.append(remote.start(arrived, arrived, (l3a, l3b), 2, sibling))

    for cp in weights[0] + l3:
        cp.wait_recv()

    @pl.loop(0, 4)
    def _(i):
        dots(i, 0)

    def local_part(k, s, u, owner):
        return pl.ds(aligned(owner * 128 + s * 64 + u * 32, 32), 32)

    def ring_owner(s, step):
        return (z + 15 - step) % 8 if s == 0 else (z + 1 + step) % 8

    streams = [(s, u) for u in range(2) for s in range(2)]
    ring = {}

    def ring_start(k):
        for s, u in streams:
            ring[k, s, u] = remote.start(
                part.at[k, local_part(k, s, u, ring_owner(s, 0)), :],
                rs.at[k, s, u, 0], (rsa, rsb), (k, s, u, 0), z_way[s],
            )

    ring_start(0)
    for cp in weights[1]:
        cp.wait_recv()

    @pl.loop(0, 4)
    def _(i):
        dots(i, 1)

    ring_start(1)
    in_copies = [
        pltpu.make_async_copy(
            turned.at[pl.ds(aligned(h * WIDTH, WIDTH), WIDTH), :],
            in_o.at[h],
            local_sem.at[9],
        )
    ]
    in_copies[0].start()
    in_sends = [
        remote.start(
            turned.at[pl.ds(aligned((1 - h) * WIDTH + i * 512, 512), 512), :],
            in_o.at[h, pl.ds(i * 512, 512), :],
            (ca, cb), i, partner,
        )
        for i in range(4)
    ]
    for step in range(1, 7):
        for k in range(2):
            for s, u in streams:
                ring[k, s, u].wait_recv()
                rs[k, s, u, step - 1] += part[k, local_part(k, s, u, ring_owner(s, step)), :]
                ring[k, s, u] = remote.start(
                    rs.at[k, s, u, step - 1], rs.at[k, s, u, step],
                    (rsa, rsb), (k, s, u, step), z_way[s],
                )

    for cp in code_parts:
        cp.wait()
    for cp in misc:
        cp.wait_recv()
    is_own = (z // 4) == h
    my_scales = jnp.where(
        is_own,
        sc[pl.ds(aligned(h * 16, 16), 16), pl.ds(row0, 128)].astype(f32),
        sc_other[:, pl.ds(row0, 128)].astype(f32),
    ).astype(bf16)
    squares = sq_mine[0:1, :] + sq_other[0:1, :]
    sq_o[...] = jnp.broadcast_to(squares, sq_o.shape)
    half_norms = (0.5 * penalty) * jnp.sqrt(squares + epsilon)
    z_rows = aligned(z * 128, 128)

    def residual(k):
        wide_codes = jnp.where(is_own, mine_codes[k].astype(f32), other_codes[k].astype(f32))
        inputs = wide_codes * spread(my_scales, k * 8 + x * 2, PIECE)
        shift = bias[:, pl.ds(aligned(h * WIDTH + k * HALF + x * PIECE, PIECE), PIECE)]
        for s, u in streams:
            ring[k, s, u].wait_recv()
            recon = rs[k, s, u, 6] + part[k, local_part(k, s, u, z), :]
            first = s * 64 + u * 32
            value = (recon + shift - inputs[first : first + 32, :]).astype(bf16)
            resid[k, pl.ds(aligned(z * 128 + first, 32), 32), pl.ds(x_cols, PIECE)] = value

    def send_x(k, owner, sems, index):
        tile = resid.at[k, pl.ds(aligned(owner * 128, 128), 128), pl.ds(x_cols, PIECE)]
        return [
            remote.start(tile, tile, sems, (index, o - 1), at(xx=xp[o])) for o in (2, 1, 3)
        ]

    def block_at(way, distance):
        return (z + 8 - distance) % 8 if way == 0 else (z + distance) % 8

    zc = {}

    def send_z(k, way, j):
        sub = j % 2 if way == 0 else 1 - j % 2
        rows = pl.ds(aligned(block_at(way, j // 2) * 128 + sub * 64, 64), 64)
        cols = pl.ds(0, HALF) if k == 0 else pl.ds(x_cols, PIECE)
        tile = resid.at[k, rows, cols]
        sems = (z0a, z0b) if k == 0 else (z1a, z1b)
        zc[k, way, j] = remote.start(tile, tile, sems, (way, j), z_way[way])

    residual(0)
    x0 = send_x(0, z, (x0a, x0b), 0)
    residual(1)
    for way in range(2):
        for j in range(2):
            send_z(1, way, j)
    order = [z, block_at(0, 1), block_at(1, 1), block_at(0, 2), block_at(1, 2), block_at(0, 3), block_at(1, 3)]
    order.append((z + 4) % 8)
    x1 = [send_x(1, z, (x1a, x1b), 0)]
    for cp in x0:
        cp.wait_recv()
    for j in range(2):
        for way in range(2):
            send_z(0, way, j)
    for j in range(7):
        for way in range(2):
            zc[1, way, j].wait_recv()
            if j + 2 < 7:
                send_z(1, way, j + 2)
            if j % 2 == 1:
                x1.append(send_x(1, order[len(x1)], (x1a, x1b), len(x1)))
    x1.append(send_x(1, order[7], (x1a, x1b), 7))

    core_rows = aligned(c * 64, 64)
    y_rows = aligned(y * 16, 16)
    gc, gy, py, pc = {}, {}, {}, {}

    def first(i):
        for cp in x1[i]:
            cp.wait_recv()
        start = order[i] * 128
        rows = pl.ds(aligned(start, 128), 128)
        grad[i] = (
            jnp.dot(resid[0, rows, :], w_t[:HALF, :], preferred_element_type=f32)
            + jnp.dot(resid[1, rows, :], w_t[HALF:, :], preferred_element_type=f32)
            + half_norms
        )
        theirs = pl.ds(aligned((1 - c) * 64, 64), 64)
        gc[i] = remote.start(grad.at[i, theirs, :], core_in.at[i], (gca, gcb), i, sibling)

    def second(i):
        gc[i].wait_recv()
        core_sum[i] = core_in[i] + grad[i, pl.ds(core_rows, 64), :]
        gy[i] = [
            remote.start(
                core_sum.at[i, pl.ds(aligned(yp[o] * 16, 16), 16), :], y_in.at[i, o - 1],
                (gya, gyb), (i, o - 1), at(yy=yp[o]),
            )
            for o in (2, 1, 3)
        ]

    def third(i):
        for cp in gy[i]:
            cp.wait_recv()
        total = core_sum[i, pl.ds(y_rows, 16), :] + y_in[i, 0] + y_in[i, 1] + y_in[i, 2]
        rows = pl.ds(aligned(order[i] * 128 + c * 64 + y * 16, 16), 16)
        active = la[rows, pl.ds(my_cols, FB)].astype(f32) > 0
        pre[rows, :] = jnp.where(active, total, 0.0).astype(bf16)
        tile = pre.at[rows, :]
        py[i] = [remote.start(tile, tile, (pya, pyb), (i, o - 1), at(yy=yp[o])) for o in (2, 1, 3)]

    def fourth(i):
        for cp in py[i]:
            cp.wait_recv()
        tile = pre.at[pl.ds(aligned(order[i] * 128 + c * 64, 64), 64), :]
        pc[i] = remote.start(tile, tile, (pca, pcb), i, sibling)

    def stages(t):
        for lag, stage in zip(LAGS, (first, second, third, fourth)):
            if 0 <= t - lag < 8:
                stage(t - lag)

    for j in range(7):
        for way in range(2):
            zc[0, way, j].wait_recv()
            if j + 2 < 7:
                send_z(0, way, j + 2)
        stages(j)
    out_copies = [
        pltpu.make_async_copy(resid, resid_o, local_sem.at[6]),
        pltpu.make_async_copy(la.at[:, pl.ds(my_cols, FB)], acts_o, local_sem.at[7]),
    ]
    for t in range(7, 8 + LAGS[-1]):
        stages(t)
        if t == 7:
            for cp in out_copies:
                cp.start()
    for cp in pc.values():
        cp.wait_recv()
    pre_o[...] = pre[...]
    for cp in in_sends:
        cp.wait_recv()
    for cp in out_copies + in_copies:
        cp.wait()
    remote.finish()


def exchange(lat, w, sc, bias, codes):
    vmem = pl.BlockSpec(memory_space=pltpu.VMEM)
    hbm = pl.BlockSpec(memory_space=pltpu.HBM)
    shape = jax.ShapeDtypeStruct
    pairs = [(3,), (2, 3), (4,), (4,), (2, 2, 2, 7), (1, 3), (2, 7), (2, 7), (8, 3), (8,), (8, 3), (8, 3), (8,), (4,), (4,)]
    return pl.pallas_call(
        exchange_kernel,
        out_shape=[
            shape((2, ROWS, HALF), bf16),
            shape((ROWS, FB), bf16),
            shape((ROWS, FB), bf16),
            shape((8, FB), f32),
            shape((2, WIDTH, ROWS // 2), bf16),
        ],
        in_specs=[hbm, hbm, vmem, vmem, hbm],
        out_specs=[hbm, hbm, vmem, vmem, hbm],
        scratch_shapes=[
            pltpu.VMEM((ROWS, 4 * FB), bf16),
            pltpu.VMEM((FB, WIDTH), bf16),
            pltpu.VMEM((2, 4 * FB, PIECE), bf16),
            pltpu.VMEM((2, ROWS, PIECE), f32),
            pltpu.VMEM((2, 2, 2, 7, 32, PIECE), f32),
            pltpu.VMEM((2, ROWS, HALF), bf16),
            pltpu.VMEM((8, 128, FB), f32),
            pltpu.VMEM((8, 64, FB), f32),
            pltpu.VMEM((8, 64, FB), f32),
            pltpu.VMEM((8, 3, 16, FB), f32),
            pltpu.VMEM((ROWS, FB), bf16),
            pltpu.VMEM((2, 128, PIECE), bf16),
            pltpu.VMEM((2, 128, PIECE), bf16),
            pltpu.VMEM((8, FB), f32),
            pltpu.VMEM((8, FB), f32),
            pltpu.VMEM((16, ROWS // 2), bf16),
            pltpu.VMEM((ROWS // 2, 2 * WIDTH), bf16),
            pltpu.VMEM((32, ROWS // 2), f32),
            pltpu.VMEM((2 * WIDTH, ROWS // 2), bf16),
            pltpu.VMEM((WIDTH, FB), bf16),
            pltpu.SemaphoreType.DMA((10,)),
        ]
        + [pltpu.SemaphoreType.DMA(count) for count in pairs for _ in range(2)],
        compiler_params=pltpu.CompilerParams(
            collective_id=0, has_side_effects=True, vmem_limit_bytes=VMEM_LIMIT
        ),
        name="exchange",
    )(lat, w, sc, bias, codes)


def grads_kernel(acts, resid, w, pre, squares, inputs, enc_o, dec_o, bias_o):
    act_sum = jnp.sum(acts[...].astype(f32), axis=0, keepdims=True)
    scale = penalty * act_sum / jnp.sqrt(squares[0:1, :] + epsilon)
    column = jnp.broadcast_to(scale, (128, 128)).T
    for k in range(2):
        term = lax.dot_general(acts[...], resid[k], TN, preferred_element_type=f32)
        for j in range(8):
            cols = slice(k * HALF + j * 128, k * HALF + j * 128 + 128)
            dec_o[pl.ds(k * 8 + j, 128, stride=16), :] = (
                term[:, j * 128 : j * 128 + 128] + column * w[:, cols].astype(f32)
            )
    enc = jnp.dot(inputs[0], pre[: ROWS // 2, :], preferred_element_type=f32)
    enc += jnp.dot(inputs[1], pre[ROWS // 2 :, :], preferred_element_type=f32)
    for j in range(4):
        enc_o[pl.ds(j, 512, stride=4), :] = enc[:, j * 128 : j * 128 + 128]

    @pl.when(pl.program_id(0) == 0)
    def _():
        bias_o[...] = jnp.sum(pre[...].astype(f32), axis=0, keepdims=True)


def grads(acts, resid, w, pre, squares, inputs):
    whole = lambda *shape: pl.BlockSpec(shape, lambda i: (0,) * len(shape))
    return pl.pallas_call(
        grads_kernel,
        grid=(4,),
        in_specs=[
            pl.BlockSpec((ROWS, 128), lambda i: (0, i)),
            whole(2, ROWS, HALF),
            pl.BlockSpec((128, WIDTH), lambda i: (i, 0)),
            whole(ROWS, FB),
            pl.BlockSpec((8, 128), lambda i: (0, i)),
            pl.BlockSpec((2, 512, ROWS // 2), lambda i: (0, i, 0)),
        ],
        out_specs=[
            pl.BlockSpec((2048, 128), lambda i: (i, 0)),
            pl.BlockSpec((2048, 128), lambda i: (i, 0)),
            whole(1, FB),
        ],
        out_shape=[
            jax.ShapeDtypeStruct((WIDTH * 4, 128), f32),
            jax.ShapeDtypeStruct((FB * 16, 128), f32),
            jax.ShapeDtypeStruct((1, FB), f32),
        ],
        compiler_params=pltpu.CompilerParams(vmem_limit_bytes=50 * 2**20),
        name="grads",
    )(acts, resid, w, pre, squares, inputs)


def shards(act_codes, act_scales, latents, dec_weight, dec_bias):
    w = dec_weight[:, 0, :]
    resid, acts, pre, squares, inputs = exchange(
        latents, w, act_scales[:, 0, :].T, dec_bias, act_codes[:, 0, :]
    )
    enc, dec, bias = grads(acts, resid, w, pre, squares, inputs)
    return enc.reshape(WIDTH, 1, FB), dec.reshape(FB, 1, WIDTH), bias.reshape(FB)


def solution(mesh):
    in_specs = (
        P("dp", "lyr", None),
        P("dp", "lyr", None),
        P("dp", "lat"),
        P("lat", "lyr", "dp"),
        P("lyr", None),
    )
    out_specs = (P("dp", "lyr", "lat"), P("lat", "lyr", "dp"), P("lat"))
    return jax.shard_map(shards, mesh=mesh, in_specs=in_specs, out_specs=out_specs, check_vma=False)
```
